32 devices in a mesh: seq: 8 (over z, y), dp: 4 (over x, core).
Axes of the slice: x: 2, y: 2, z: 4, core: 2. Of those that a mesh axis runs over, the one named last changes fastest.
Arguments:
- bases: int32 [98304], P(('dp', 'seq')), parts along dimension 0, may hold values from 0 to 3
- stem_weight: bfloat16 [20, 768], replicated, may hold values from -3 to 3
- stem_gain: float32 [768], replicated, may hold values from 0.5 to 1.5
- first_weight: bfloat16 [5, 768, 896], P(None, None, 'seq'), may hold values from -0.09375 to 0.09375
- first_gain: float32 [896], replicated, may hold values from 0.5 to 1.5
- second_weight: bfloat16 [5, 896, 1024], P(None, None, 'seq'), may hold values from -0.09375 to 0.09375
- second_gain: float32 [1024], replicated, may hold values from 0.5 to 1.5
- bottom_project: bfloat16 [1024, 1024], P(None, 'seq'), may hold values from -0.1875 to 0.1875
- middle_project: bfloat16 [1024, 896], P(None, 'seq'), may hold values from -0.1875 to 0.1875
- top_project: bfloat16 [896, 768], P(None, 'seq'), may hold values from -0.1875 to 0.1875
- head_weight: bfloat16 [768, 5], replicated, may hold values from -0.21875 to 0.21875
Outputs:
- features: bfloat16 [98304, 768], P(('dp', 'seq')), parts along dimension 0
- splice_logits: float32 [5, 98304], P(None, ('dp', 'seq')), parts along dimension 1
The draws below stay inside these ranges and needn't reach their ends.
There are 4 independent parts, one for each index of `dp`. The reference program is written for one: setup_inputs(seed, part) draws one part's arguments, and reference() takes and returns one part's arrays. A program takes and returns all parts, laid end to end along the dimension named above; an argument that names none is the same for every part. Nothing has to cross between parts.
All inputs are finite; a program needn't handle non-finite values.
Results may differ from the reference program's by a relative error of at most 0.015.
Values may be sent and summed in bfloat16 or wider, within the bound.
A program may use at most 192 MiB of HBM per device.

```python
import jax
import jax.numpy as jnp
from jax import lax

C0 = 768
C1 = 896
C2 = 1024
CLASSES = 5
TAPS = 5
LENGTH = 24576


def plant(drawn, key, smallest, largest):
    extent = drawn.shape
    place = [jax.random.randint(jax.random.fold_in(key, axis), (), 0, extent[axis]) for axis in range(len(extent))]
    drawn = drawn.at[tuple(place)].set(smallest)
    longest = extent.index(max(extent))
    place[longest] = (place[longest] + 1) % extent[longest]
    return drawn.at[tuple(place)].set(largest)


def level_of(rng, shape, cuts, smallest, largest):
    def one(dim, shards_of):
        draws = jax.random.uniform(jax.random.fold_in(jax.random.fold_in(rng, 6), dim), (shards_of,), jnp.float32, smallest / len(cuts), largest / len(cuts))
        return jnp.repeat(jnp.exp(draws), shape[dim] // shards_of).reshape((-1,) + (1,) * (len(shape) - dim - 1))

    level = one(*cuts[0])
    for cut in cuts[1:]:
        level = level * one(*cut)
    return level


def centred(rng, extent, width, most, pieces=(), kind=jnp.bfloat16):
    factor_of = level_of(rng, extent, pieces, -0.22, 0.18) if pieces else 1.0
    array = jax.random.normal(rng, extent, jnp.float32) * width * factor_of
    return jnp.minimum(jnp.maximum(array, -most), most).astype(kind)


def setup_inputs(seed: int = 0, part: int = 0) -> dict:
    key_of = jax.random.split(jax.random.key(seed), 12)
    part_keys = jax.random.split(jax.random.fold_in(key_of[11], part), 12)
    return {
        "bases": plant(jax.random.randint(part_keys[0], (LENGTH,), 0, 4), jax.random.fold_in(part_keys[0], 1), 0, 3).astype(jnp.int32),
        "stem_weight": centred(key_of[1], (4 * TAPS, C0), 0.5, 3.0),
        "stem_gain": jnp.clip(jax.random.uniform(key_of[2], (C0,), jnp.float32, 0.5, 1.5), 0.5, 1.5),
        "first_weight": centred(key_of[3], (TAPS, C0, C1), (TAPS * C0) ** -0.5, 0.09375, ((2, 8),)),
        "first_gain": jnp.clip(jax.random.uniform(key_of[4], (C1,), jnp.float32, 0.5, 1.5), 0.5, 1.5),
        "second_weight": centred(key_of[5], (TAPS, C1, C2), (TAPS * C1) ** -0.5, 0.09375, ((2, 8),)),
        "second_gain": jnp.clip(jax.random.uniform(key_of[6], (C2,), jnp.float32, 0.5, 1.5), 0.5, 1.5),
        "bottom_project": centred(key_of[7], (C2, C2), C2 ** -0.5, 0.1875, ((1, 8),)),
        "middle_project": centred(key_of[8], (C2, C1), C2 ** -0.5, 0.1875, ((1, 8),)),
        "top_project": centred(key_of[9], (C1, C0), C1 ** -0.5, 0.1875, ((1, 8),)),
        "head_weight": centred(key_of[10], (C0, CLASSES), C0 ** -0.5, 0.21875),
    }


def convolve(rows, weight):
    length = rows.shape[0]
    padded = jnp.pad(rows, ((2, 2), (0, 0)))
    total = jnp.zeros((length, weight.shape[2]), jnp.float32)
    for tap_index in range(5):
        total = total + jnp.dot(padded[tap_index:tap_index + length], weight[tap_index], preferred_element_type=jnp.float32)
    return total

def activate(values, gain):
    mean_square = lax.optimization_barrier(jnp.mean(values * values, axis=1, keepdims=True))
    activated = jax.nn.gelu(values * lax.rsqrt(mean_square + 1e-06) * gain.astype(jnp.float32), approximate=True)
    skip = activated.astype(jnp.bfloat16)
    pooled = (0.5 * (activated[0::2] + activated[1::2])).astype(jnp.bfloat16)
    return (skip, pooled)

def reference(bases, stem_weight, stem_gain, first_weight, first_gain, second_weight, second_gain, bottom_project, middle_project, top_project, head_weight):
    length = bases.shape[0]
    padded = jnp.pad(bases, 2, constant_values=-1)
    windows = jnp.stack([padded[tap_index:tap_index + length] for tap_index in range(5)], axis=1)
    letters = jnp.arange(4, dtype=jnp.int32)
    onehot = (windows[:, :, None] == letters[None, None, :]).reshape(length, 20).astype(jnp.float32)
    stem_out = jnp.dot(onehot, stem_weight.astype(jnp.float32), preferred_element_type=jnp.float32)
    skip_zero, pooled_one = activate(stem_out, stem_gain)
    skip_one, pooled_two = activate(convolve(pooled_one, first_weight), first_gain)
    skip_two, pooled_three = activate(convolve(pooled_two, second_weight), second_gain)
    upward = pooled_three
    for skip, project in ((skip_two, bottom_project), (skip_one, middle_project), (skip_zero, top_project)):
        lifted = jnp.dot(upward, project, preferred_element_type=jnp.float32)
        upward = (skip.astype(jnp.float32) + jnp.repeat(lifted, 2, axis=0)).astype(jnp.bfloat16)
    logits = jnp.dot(upward.astype(jnp.float32), head_weight.astype(jnp.float32), preferred_element_type=jnp.float32).T
    return (upward, logits)
```

```python
import functools

import jax
import jax.numpy as jnp
from jax import lax
from jax.experimental import pallas as pl
from jax.experimental.pallas import tpu as pltpu
from jax.sharding import PartitionSpec as P

TAPS = 5
CLASSES = 8
HALO = 16
CHUNK = 32
LANES = 128
PIECE = 1024
BF16 = jnp.bfloat16
F32 = jnp.float32


def gather_kernel(pieces, x_ref, g_ref, local_sem, nat_recv, x_recv, ca_recv, cb_recv,
                  own_send, nat_send, x_send, ca_send, cb_send):
    seq = lax.axis_index("seq")
    dp = lax.axis_index("dp")
    z, y = seq // 2, seq % 2
    x, c = dp // 2, dp % 2
    half, edge, native = PIECE // 2, 3 * PIECE // 16, 5 * PIECE // 16

    def there(zz, yy, xx, cc):
        return {"seq": zz * 2 + yy, "dp": xx * 2 + cc}

    y_dev = there(z, 1 - y, x, c)
    x_dev = there(z, y, 1 - x, c)
    c_dev = there(z, y, x, 1 - c)
    up_dev = there(jnp.minimum(z + 1, 3), y, x, c)
    down_dev = there(jnp.maximum(z - 1, 0), y, x, c)

    barrier = pltpu.get_barrier_semaphore()
    for dev in (y_dev, x_dev, c_dev):
        pl.semaphore_signal(barrier, inc=1, device_id=dev, device_id_type=pl.DeviceIdType.MESH)

    @pl.when(z < 3)
    def _():
        pl.semaphore_signal(barrier, inc=1, device_id=up_dev, device_id_type=pl.DeviceIdType.MESH)

    @pl.when(z > 0)
    def _():
        pl.semaphore_signal(barrier, inc=1, device_id=down_dev, device_id_type=pl.DeviceIdType.MESH)

    inner = jnp.logical_and(z > 0, z < 3)

    @pl.when(inner)
    def _():
        pl.semaphore_wait(barrier, 5)

    @pl.when(jnp.logical_not(inner))
    def _():
        pl.semaphore_wait(barrier, 4)

    def slot(zz, yy, start, count):
        return g_ref.at[zz, pl.ds(pl.multiple_of(start, 64), count),
                        pl.ds(pl.multiple_of(yy * LANES, LANES), LANES)]

    def base(k):
        return k * PIECE + c * half

    def copy(src, dst, send, recv, dev):
        return pltpu.make_async_remote_copy(src_ref=src, dst_ref=dst, send_sem=send, recv_sem=recv,
                                            device_id=dev, device_id_type=pl.DeviceIdType.MESH)

    def nat(k, zz, yy):
        return slot(zz, yy, base(k) + x * edge, native)

    def part(k, zz, yy, xx):
        return slot(zz, yy, base(k) + xx * native, edge)

    def own_copy(k, dev, which):
        src = x_ref.at[pl.ds(pl.multiple_of(base(k) + x * edge, 64), native), :]
        return copy(src, nat(k, z, y), own_send.at[k, which], nat_recv.at[k, seq], dev)

    def z_copy(k, zz, dev):
        s = zz * 2 + y
        return copy(nat(k, zz, y), nat(k, zz, y), nat_send.at[k, 0, zz], nat_recv.at[k, s], dev)

    def y_copy(k, zz):
        s = zz * 2 + y
        return copy(nat(k, zz, y), nat(k, zz, y), nat_send.at[k, 1, zz], nat_recv.at[k, s], y_dev)

    def x_copy(k, zz, yy):
        s = zz * 2 + yy
        return copy(part(k, zz, yy, x), part(k, zz, yy, x), x_send.at[k, s], x_recv.at[k, s], x_dev)

    def ca_copy(k, zz, yy):
        s = zz * 2 + yy
        return copy(nat(k, zz, yy), nat(k, zz, yy), ca_send.at[k, s], ca_recv.at[k, s], c_dev)

    def cb_copy(k, zz, yy):
        s = zz * 2 + yy
        return copy(part(k, zz, yy, 1 - x), part(k, zz, yy, 1 - x), cb_send.at[k, s], cb_recv.at[k, s], c_dev)

    local = pltpu.make_async_copy(
        x_ref, g_ref.at[z, :, pl.ds(pl.multiple_of(y * LANES, LANES), LANES)], local_sem)
    local.start()

    def wait_nat(k, zz, yy):
        pltpu.make_async_copy(nat(k, zz, yy), nat(k, zz, yy), nat_recv.at[k, zz * 2 + yy]).wait()

    def wait_part(k, zz, yy, sem):
        ref = part(k, zz, yy, 1 - x)
        pltpu.make_async_copy(ref, ref, sem.at[k, zz * 2 + yy]).wait()

    def over(body):
        def step(k, carry):
            body(k)
            return carry
        lax.fori_loop(0, pieces, step, 0)

    def when(cond):
        return pl.when(cond)

    def first(k):
        when(z < 3)(lambda: own_copy(k, up_dev, 0).start())
        when(z > 0)(lambda: own_copy(k, down_dev, 1).start())
        own_copy(k, y_dev, 2).start()

    over(first)

    for phase in range(1, 6):
        def body(k, phase=phase):
            if phase <= 3:
                for sign in (-1, 1):
                    zz = z + sign * phase

                    @pl.when(jnp.logical_and(zz >= 0, zz < 4))
                    def _(zz=zz, sign=sign):
                        wait_nat(k, zz, y)
                        if sign < 0:
                            when(z < 3)(lambda: z_copy(k, zz, up_dev).start())
                        else:
                            when(z > 0)(lambda: z_copy(k, zz, down_dev).start())
                        y_copy(k, zz).start()
                        x_copy(k, zz, y).start()
                        ca_copy(k, zz, y).start()
            if phase <= 4:
                for sign in (-1, 1) if phase > 1 else (1,):
                    zz = z + sign * (phase - 1)

                    @pl.when(jnp.logical_and(zz >= 0, zz < 4))
                    def _(zz=zz):
                        wait_nat(k, zz, 1 - y)
                        x_copy(k, zz, 1 - y).start()
                        ca_copy(k, zz, 1 - y).start()
            late = []
            if 2 <= phase <= 4:
                late += [(z - (phase - 1), y), (z + (phase - 1), y)]
            if phase == 2:
                late += [(z, 1 - y)]
            if phase > 2:
                late += [(z - (phase - 2), 1 - y), (z + (phase - 2), 1 - y)]
            for zz, yy in late:
                @pl.when(jnp.logical_and(zz >= 0, zz < 4))
                def _(zz=zz, yy=yy):
                    wait_part(k, zz, yy, x_recv)
                    cb_copy(k, zz, yy).start()

        over(body)

    def last(k):
        when(z < 3)(lambda: own_copy(k, up_dev, 0).wait_send())
        when(z > 0)(lambda: own_copy(k, down_dev, 1).wait_send())
        own_copy(k, y_dev, 2).wait_send()
        for zz in range(4):
            @pl.when(zz != z)
            def _(zz=zz):
                when(jnp.logical_and(zz < z, z < 3))(lambda: z_copy(k, zz, up_dev).wait_send())
                when(jnp.logical_and(zz > z, z > 0))(lambda: z_copy(k, zz, down_dev).wait_send())
                y_copy(k, zz).wait_send()
            for yy in range(2):
                @pl.when(zz * 2 + yy != seq)
                def _(zz=zz, yy=yy):
                    x_copy(k, zz, yy).wait_send()
                    ca_copy(k, zz, yy).wait_send()
                    cb_copy(k, zz, yy).wait_send()
                    start = k * PIECE + (1 - c) * half
                    got = slot(zz, yy, start + x * edge, native)
                    pltpu.make_async_copy(got, got, ca_recv.at[k, zz * 2 + yy]).wait()
                    got = slot(zz, yy, start + (1 - x) * native, edge)
                    pltpu.make_async_copy(got, got, cb_recv.at[k, zz * 2 + yy]).wait()

    over(last)
    local.wait()


def gather_shards(shard):
    rows = shard.shape[0]
    pieces = rows // PIECE
    dma = pltpu.SemaphoreType.DMA
    return pl.pallas_call(
        functools.partial(gather_kernel, pieces),
        out_shape=jax.ShapeDtypeStruct((4, rows, 2 * LANES), shard.dtype),
        in_specs=[pl.BlockSpec(memory_space=pl.ANY)],
        out_specs=pl.BlockSpec(memory_space=pl.ANY),
        scratch_shapes=[dma, dma((pieces, 8)), dma((pieces, 8)), dma((pieces, 8)), dma((pieces, 8)),
                        dma((pieces, 3)), dma((pieces, 2, 4)), dma((pieces, 8)), dma((pieces, 8)), dma((pieces, 8))],
        compiler_params=pltpu.CompilerParams(collective_id=0, has_side_effects=True,
                                             vmem_limit_bytes=16 * 1024 * 1024),
        cost_estimate=pl.CostEstimate(flops=0, bytes_accessed=60_000_000, transcendentals=0),
        name="gather",
    )(shard)


def gelu_norm(values, gain, width):
    square = jnp.sum(values * values, axis=1, keepdims=True) * (1.0 / width)
    v = values * lax.rsqrt(square + 1e-06) * gain
    u = v * (0.7978845608028654 + (0.7978845608028654 * 0.044715) * (v * v))
    h = 0.5 * v
    return h + h * jnp.tanh(u)


def unet_kernel(dims, g_ref, hot_ref, sw_ref, mask_ref, gain0_ref, gain1_ref, gain2_ref, head_ref,
                out_ref, logit_ref, gv, sems, wide, pf, pb1, pb2, skip0, skip1, skip2, mix):
    rows, c0, c1, c2, offs = dims
    ext = rows + 2 * HALO
    w0, w1 = c0 // 8, c1 // 8
    cuts = list(zip(offs[:-1], offs[1:]))

    def load(n):
        lo, hi = cuts[n]
        return pltpu.make_async_copy(g_ref.at[:, pl.ds(lo, hi - lo), :], gv.at[:, pl.ds(lo, hi - lo), :], sems.at[n])

    for n in range(5):
        load(n).start()

    def chunks(count, body):
        def step(i, carry):
            body(pl.multiple_of(i * CHUNK, CHUNK))
            return carry
        lax.fori_loop(0, count // CHUNK, step, 0)

    def shifted(k, start, shift, width):
        if shift == 0:
            return pf[k, pl.ds(start, CHUNK), 0:width].astype(BF16)
        if shift < 0:
            return pf[k, pl.ds(start - 8, CHUNK + 8), 0:width][7:7 + CHUNK].astype(BF16)
        return pf[k, pl.ds(start, CHUNK + 8), 0:width][1:1 + CHUNK].astype(BF16)

    zeros = jnp.zeros((8, pf.shape[2]), F32)
    for k in range(4):
        pf[k, 0:8, :] = zeros
        pf[k, 8 + ext:16 + ext, :] = zeros

    def stem(j, carry):
        for e in range(2):
            wide[e, :, 0:c0] = jnp.dot(hot_ref[...], sw_ref[2 * j + e], preferred_element_type=F32)

        def body(r):
            a0 = gelu_norm(wide[0, pl.ds(r, CHUNK), 0:c0], gain0_ref[...], c0)
            a1 = gelu_norm(wide[1, pl.ds(r, CHUNK), 0:c0], gain0_ref[...], c0)
            skip0[2 * j, pl.ds(r, CHUNK), :] = a0.astype(BF16)
            skip0[2 * j + 1, pl.ds(r, CHUNK), :] = a1.astype(BF16)
            pf[j, pl.ds(r + 8, CHUNK), 0:c0] = 0.5 * (a0 + a1) * mask_ref[pl.ds(r, CHUNK), 0:1]

        chunks(ext, body)
        return carry

    lax.fori_loop(0, 4, stem, 0)

    where1 = {(k, 0): k for k in range(4)} | {(2, -1): 4, (3, -1): 5, (0, 1): 6, (1, 1): 7}
    for (k, shift), at in where1.items():
        def body(r, k=k, shift=shift, at=at):
            pb1[at, pl.ds(r, CHUNK), :] = shifted(k, r + 8, shift, c0)
        chunks(ext, body)

    load(0).wait()
    for j in range(2):
        for e in range(2):
            k = 2 * j + e

            def column(p, carry, k=k, e=e):
                acc = None
                for t in range(TAPS):
                    shift, cls = divmod(k + t - 2, 4)
                    term = jnp.dot(pb1[where1[(cls, shift)]], gv[p, offs[0] + t * c0:offs[0] + (t + 1) * c0, :],
                                   preferred_element_type=F32)
                    acc = term if acc is None else acc + term
                wide[e, :, pl.ds(pl.multiple_of(p * 256, 256), 256)] = acc
                return carry

            lax.fori_loop(0, 4, column, 0)

        def body(r, j=j):
            both = []
            for e in range(2):
                row = wide[e, pl.ds(r, CHUNK), :]
                row = jnp.concatenate([row[:, s * LANES:s * LANES + w1] for s in range(8)], axis=1)
                a = gelu_norm(row, gain1_ref[...], c1)
                skip1[2 * j + e, pl.ds(r, CHUNK), :] = a.astype(BF16)
                both.append(a)
            pf[j, pl.ds(r + 8, CHUNK), 0:c1] = 0.5 * (both[0] + both[1]) * mask_ref[pl.ds(r, CHUNK), 0:1]

        chunks(ext, body)

    where2 = {}
    for k in range(2):
        for shift in (-1, 0, 1):
            at = len(where2)
            where2[(k, shift)] = at

            def body(r, k=k, shift=shift, at=at):
                pb2[at, pl.ds(r, CHUNK), :] = shifted(k, r + 8 + HALO, shift, c1)

            chunks(rows, body)

    load(1).wait()
    for e in range(2):
        def column(p, carry, e=e):
            acc = None
            for t in range(TAPS):
                shift, cls = divmod(e + t - 2, 2)
                term = jnp.dot(pb2[where2[(cls, shift)]], gv[p, offs[1] + t * c1:offs[1] + (t + 1) * c1, :],
                               preferred_element_type=F32)
                acc = term if acc is None else acc + term
            wide[e, 0:rows, pl.ds(pl.multiple_of(p * 256, 256), 256)] = acc
            return carry

        lax.fori_loop(0, 4, column, 0)

    def body(r):
        a0 = gelu_norm(wide[0, pl.ds(r, CHUNK), :], gain2_ref[...], c2)
        a1 = gelu_norm(wide[1, pl.ds(r, CHUNK), :], gain2_ref[...], c2)
        skip2[0, pl.ds(r, CHUNK), :] = a0.astype(BF16)
        skip2[1, pl.ds(r, CHUNK), :] = a1.astype(BF16)
        skip2[2, pl.ds(r, CHUNK), :] = (0.5 * (a0 + a1)).astype(BF16)

    chunks(rows, body)

    def lift(slot, lhs, n, depth):
        def column(p, carry):
            wide[slot, 0:rows, pl.ds(pl.multiple_of(p * 256, 256), 256)] = jnp.dot(
                lhs(), gv[p, offs[n]:offs[n] + depth, :], preferred_element_type=F32)
            return carry
        lax.fori_loop(0, 4, column, 0)

    load(2).wait()
    lift(0, lambda: skip2[2], 2, c2)

    def body(r):
        up = wide[0, pl.ds(r, CHUNK), :]
        for e in range(2):
            skip2[e, pl.ds(r, CHUNK), :] = (skip2[e, pl.ds(r, CHUNK), :].astype(F32) + up).astype(BF16)

    chunks(rows, body)

    load(3).wait()

    def middle(j, carry):
        lift(0, lambda: skip2[j], 3, c2)

        def body(r):
            row = wide[0, pl.ds(r, CHUNK), :]
            up = jnp.concatenate([row[:, s * LANES:s * LANES + w1] for s in range(8)], axis=1)
            for e in range(2):
                at = pl.ds(r + HALO, CHUNK)
                skip1[2 * j + e, at, :] = (skip1[2 * j + e, at, :].astype(F32) + up).astype(BF16)

        chunks(rows, body)
        return carry

    lax.fori_loop(0, 2, middle, 0)

    load(4).wait()

    def top(j, carry):
        lift(0, lambda: skip1[j, HALO:HALO + rows, :], 4, c1)

        def body(r):
            row = wide[0, pl.ds(r, CHUNK), :]
            up = jnp.concatenate([row[:, s * LANES:s * LANES + w0] for s in range(8)], axis=1)
            pf[j, pl.ds(r, CHUNK), 0:c0] = up

        chunks(rows, body)
        return carry

    lax.fori_loop(0, 4, top, 0)

    def final(i, carry):
        r = pl.multiple_of(i * 16, 16)
        for j in range(4):
            up = pf[j, pl.ds(r, 16), 0:c0]
            for e in range(2):
                k = 2 * j + e
                f = skip0[k, pl.ds(r + HALO, 16), :].astype(F32) + up
                for lane in range(0, c0, LANES):
                    mix[lane // LANES, pl.ds(k, 16, stride=8), :] = f[:, lane:lane + LANES]
        o = pl.multiple_of(i * 128, 128)
        for lane in range(0, c0, LANES):
            out_ref[pl.ds(o, 128), lane:lane + LANES] = mix[lane // LANES].astype(BF16)
        logits = lax.dot_general(head_ref[...], out_ref[pl.ds(o, 128), :], (((1,), (1,)), ((), ())),
                                 preferred_element_type=F32)
        logit_ref[:, pl.ds(o, 128)] = logits[0:logit_ref.shape[0]]
        return carry

    lax.fori_loop(0, rows // 16, final, 0)


def unet(g, hot, sw, mask, gain0, gain1, gain2, head, dims, classes):
    rows, c0, c1, c2, offs = dims
    ext = rows + 2 * HALO
    vmem = pl.BlockSpec(memory_space=pltpu.VMEM)
    head = jnp.pad(head.T, ((0, 16 - classes), (0, 0)))
    return pl.pallas_call(
        functools.partial(unet_kernel, dims),
        out_shape=(jax.ShapeDtypeStruct((rows * 8, c0), BF16), jax.ShapeDtypeStruct((classes, rows * 8), F32)),
        in_specs=[pl.BlockSpec(memory_space=pl.ANY)] + [vmem] * 7,
        out_specs=(vmem, vmem),
        scratch_shapes=[
            pltpu.VMEM(g.shape, BF16),
            pltpu.SemaphoreType.DMA((5,)),
            pltpu.VMEM((2, ext, 1024), F32),
            pltpu.VMEM((4, ext + 16, c1), F32),
            pltpu.VMEM((8, ext, c0), BF16),
            pltpu.VMEM((6, rows, c1), BF16),
            pltpu.VMEM((8, ext, c0), BF16),
            pltpu.VMEM((4, ext, c1), BF16),
            pltpu.VMEM((3, rows, c2), BF16),
            pltpu.VMEM((c0 // LANES, 128, LANES), F32),
        ],
        compiler_params=pltpu.CompilerParams(vmem_limit_bytes=64 * 1024 * 1024 - 512 * 1024),
        name="unet",
    )(g, hot, sw, mask, gain0[None], gain1[None], gain2[None], head)


def flat(weight):
    weight = weight.reshape(-1, weight.shape[-1])
    return jnp.pad(weight, ((0, 0), (0, LANES - weight.shape[-1])))


def solution(mesh):
    chips = mesh.shape["seq"] == 8 and mesh.shape["dp"] == 4

    def on_device(bases, stem_weight, stem_gain, first_weight, first_gain, second_weight, second_gain,
                  bottom_project, middle_project, top_project, head_weight):
        weights = (first_weight, second_weight, bottom_project, middle_project, top_project)
        depths = [w.size // w.shape[-1] for w in weights]
        offs = [0]
        for d in depths:
            offs.append(offs[-1] + d)
        if chips and offs[-1] % PIECE == 0:
            g = gather_shards(jnp.concatenate([flat(w) for w in weights], axis=0))
        else:
            parts = []
            for w in weights:
                whole = lax.all_gather(w.reshape(-1, w.shape[-1]), "seq", axis=1, tiled=True)
                whole = whole.reshape(whole.shape[0], 8, -1)
                whole = jnp.pad(whole, ((0, 0), (0, 0), (0, LANES - whole.shape[2])))
                parts.append(whole.reshape(-1, 4, 2 * LANES).transpose(1, 0, 2))
            g = jnp.concatenate(parts, axis=1)

        count = lax.axis_size("seq")
        me = lax.axis_index("seq")
        length = bases.shape[0]
        rows = length // CLASSES
        ext = rows + 2 * HALO
        forward = [(i, i + 1) for i in range(count - 1)]
        low = lax.ppermute(bases[-16:] + 1, "seq", forward) - 1
        high = lax.ppermute(bases[:16] + 1, "seq", [(b, a) for a, b in forward]) - 1
        blank = jnp.full((8 * (HALO + 1) - 16,), -1, jnp.int32)
        line = jnp.concatenate([blank, low, bases, high, blank]).reshape(ext + 2, 8)
        window = jnp.concatenate([line[:-2, 6:], line[1:-1], line[2:, :2]], axis=1)
        lane = jnp.arange(48, dtype=jnp.int32)
        hot = (jnp.repeat(window, 4, axis=1) == (lane % 4)[None]).astype(BF16)
        sw = jnp.stack([jnp.pad(stem_weight, ((4 * r, 28 - 4 * r), (0, 0))) for r in range(8)])
        q = jnp.arange(ext)[:, None]
        outside = ((me == 0) & (q < HALO)) | ((me == count - 1) & (q >= HALO + rows))
        mask = jnp.broadcast_to(jnp.where(outside, 0.0, 1.0).astype(F32), (ext, LANES))
        dims = (rows, stem_weight.shape[1], first_gain.shape[0], second_gain.shape[0], tuple(offs))
        return unet(g, hot, sw, mask, stem_gain, first_gain, second_gain, head_weight, dims, head_weight.shape[1])

    placed = (
        P(("dp", "seq")),
        P(),
        P(),
        P(None, None, "seq"),
        P(),
        P(None, None, "seq"),
        P(),
        P(None, "seq"),
        P(None, "seq"),
        P(None, "seq"),
        P(),
    )
    return jax.shard_map(
        on_device,
        mesh=mesh,
        in_specs=placed,
        out_specs=(P(("dp", "seq"), None), P(None, ("dp", "seq"))),
        check_vma=False,
    )
```

```python
import functools

import jax
import jax.numpy as jnp
from jax import lax
from jax.experimental import pallas as pl
from jax.experimental.pallas import tpu as pltpu
from jax.sharding import PartitionSpec as P

TAPS = 5
CLASSES = 8
HALO = 16
CHUNK = 32
LANES = 128
PIECE = 1024
BF16 = jnp.bfloat16
F32 = jnp.float32


def link_steps(pieces, x_ref, g_ref, sems):
    (local_sem, nat_recv, x_recv, ca_recv, cb_recv, own_send, nat_send, x_send, ca_send, cb_send) = sems
    seq = lax.axis_index("seq")
    dp = lax.axis_index("dp")
    z, y = seq // 2, seq % 2
    x, c = dp // 2, dp % 2
    half, edge, native = PIECE // 2, 3 * PIECE // 16, 5 * PIECE // 16

    def there(zz, yy, xx, cc):
        return {"seq": zz * 2 + yy, "dp": xx * 2 + cc}

    y_dev = there(z, 1 - y, x, c)
    x_dev = there(z, y, 1 - x, c)
    c_dev = there(z, y, x, 1 - c)
    up_dev = there(jnp.minimum(z + 1, 3), y, x, c)
    down_dev = there(jnp.maximum(z - 1, 0), y, x, c)

    barrier = pltpu.get_barrier_semaphore()
    for dev in (y_dev, x_dev, c_dev):
        pl.semaphore_signal(barrier, inc=1, device_id=dev, device_id_type=pl.DeviceIdType.MESH)

    @pl.when(z < 3)
    def _():
        pl.semaphore_signal(barrier, inc=1, device_id=up_dev, device_id_type=pl.DeviceIdType.MESH)

    @pl.when(z > 0)
    def _():
        pl.semaphore_signal(barrier, inc=1, device_id=down_dev, device_id_type=pl.DeviceIdType.MESH)

    inner = jnp.logical_and(z > 0, z < 3)

    @pl.when(inner)
    def _():
        pl.semaphore_wait(barrier, 5)

    @pl.when(jnp.logical_not(inner))
    def _():
        pl.semaphore_wait(barrier, 4)

    def slot(zz, yy, start, count):
        return g_ref.at[zz, pl.ds(pl.multiple_of(start, 64), count),
                        pl.ds(pl.multiple_of(yy * LANES, LANES), LANES)]

    def base(k):
        return k * PIECE + c * half

    def copy(src, dst, send, recv, dev):
        return pltpu.make_async_remote_copy(src_ref=src, dst_ref=dst, send_sem=send, recv_sem=recv,
                                            device_id=dev, device_id_type=pl.DeviceIdType.MESH)

    def nat(k, zz, yy):
        return slot(zz, yy, base(k) + x * edge, native)

    def part(k, zz, yy, xx):
        return slot(zz, yy, base(k) + xx * native, edge)

    def own_copy(k, dev, which):
        src = x_ref.at[pl.ds(pl.multiple_of(base(k) + x * edge, 64), native), :]
        return copy(src, nat(k, z, y), own_send.at[k, which], nat_recv.at[k, seq], dev)

    def z_copy(k, zz, dev):
        s = zz * 2 + y
        return copy(nat(k, zz, y), nat(k, zz, y), nat_send.at[k, 0, zz], nat_recv.at[k, s], dev)

    def y_copy(k, zz):
        s = zz * 2 + y
        return copy(nat(k, zz, y), nat(k, zz, y), nat_send.at[k, 1, zz], nat_recv.at[k, s], y_dev)

    def x_copy(k, zz, yy):
        s = zz * 2 + yy
        return copy(part(k, zz, yy, x), part(k, zz, yy, x), x_send.at[k, s], x_recv.at[k, s], x_dev)

    def ca_copy(k, zz, yy):
        s = zz * 2 + yy
        return copy(nat(k, zz, yy), nat(k, zz, yy), ca_send.at[k, s], ca_recv.at[k, s], c_dev)

    def cb_copy(k, zz, yy):
        s = zz * 2 + yy
        return copy(part(k, zz, yy, 1 - x), part(k, zz, yy, 1 - x), cb_send.at[k, s], cb_recv.at[k, s], c_dev)

    local = pltpu.make_async_copy(
        x_ref, g_ref.at[z, :, pl.ds(pl.multiple_of(y * LANES, LANES), LANES)], local_sem)
    local.start()

    def wait_nat(k, zz, yy):
        pltpu.make_async_copy(nat(k, zz, yy), nat(k, zz, yy), nat_recv.at[k, zz * 2 + yy]).wait()

    def wait_part(k, zz, yy, sem):
        ref = part(k, zz, yy, 1 - x)
        pltpu.make_async_copy(ref, ref, sem.at[k, zz * 2 + yy]).wait()

    def start_own(k):
        pl.when(z < 3)(lambda: own_copy(k, up_dev, 0).start())
        pl.when(z > 0)(lambda: own_copy(k, down_dev, 1).start())
        own_copy(k, y_dev, 2).start()

    def serve(m):
        n, i = m // 6, m % 6
        phase = (6 - i) % 6
        k = n - phase - jnp.minimum(phase, 1)

        def inside(zz):
            return jnp.logical_and(zz >= 0, zz < 4)

        @pl.when(jnp.logical_and(k >= 0, k < pieces))
        def _():
            @pl.when(phase == 0)
            def _():
                start_own(k)

            @pl.when(phase > 0)
            def _():
                for sign in (-1, 1):
                    zz = z + sign * phase

                    @pl.when(inside(zz))
                    def _(zz=zz, sign=sign):
                        wait_nat(k, zz, y)
                        if sign < 0:
                            pl.when(z < 3)(lambda: z_copy(k, zz, up_dev).start())
                        else:
                            pl.when(z > 0)(lambda: z_copy(k, zz, down_dev).start())
                        y_copy(k, zz).start()
                        x_copy(k, zz, y).start()
                        ca_copy(k, zz, y).start()
                for sign in (-1, 1):
                    zz = z + sign * (phase - 1)

                    @pl.when(jnp.logical_and(inside(zz), phase > (1 if sign < 0 else 0)))
                    def _(zz=zz):
                        wait_nat(k, zz, 1 - y)
                        x_copy(k, zz, 1 - y).start()
                        ca_copy(k, zz, 1 - y).start()
                for sign in (-1, 1):
                    zz = z + sign * (phase - 1)

                    @pl.when(jnp.logical_and(inside(zz), phase > 1))
                    def _(zz=zz):
                        wait_part(k, zz, y, x_recv)
                        cb_copy(k, zz, y).start()
                for sign in (-1, 1):
                    zz = z + sign * (phase - 2)

                    @pl.when(jnp.logical_and(inside(zz), phase > (2 if sign < 0 else 1)))
                    def _(zz=zz):
                        wait_part(k, zz, 1 - y, x_recv)
                        cb_copy(k, zz, 1 - y).start()

    def finish(lo, hi):
        def step(k, carry):
            def shard(s, carry):
                @pl.when(s != seq)
                def _():
                    zz, yy = s // 2, s % 2
                    start = k * PIECE + (1 - c) * half
                    got = slot(zz, yy, start + x * edge, native)
                    pltpu.make_async_copy(got, got, ca_recv.at[k, s]).wait()
                    got = slot(zz, yy, start + (1 - x) * native, edge)
                    pltpu.make_async_copy(got, got, cb_recv.at[k, s]).wait()
                return carry
            return lax.fori_loop(0, 8, shard, carry)
        lax.fori_loop(lo, hi, step, 0)

    def close():
        def step(k, carry):
            pl.when(z < 3)(lambda: own_copy(k, up_dev, 0).wait_send())
            pl.when(z > 0)(lambda: own_copy(k, down_dev, 1).wait_send())
            own_copy(k, y_dev, 2).wait_send()

            def shard(s, carry):
                zz, yy = s // 2, s % 2

                @pl.when(s != seq)
                def _():
                    x_copy(k, zz, yy).wait_send()
                    ca_copy(k, zz, yy).wait_send()
                    cb_copy(k, zz, yy).wait_send()

                @pl.when(jnp.logical_and(zz != z, yy == 0))
                def _():
                    pl.when(jnp.logical_and(zz < z, z < 3))(lambda: z_copy(k, zz, up_dev).wait_send())
                    pl.when(jnp.logical_and(zz > z, z > 0))(lambda: z_copy(k, zz, down_dev).wait_send())
                    y_copy(k, zz).wait_send()
                return carry
            return lax.fori_loop(0, 8, shard, carry)
        lax.fori_loop(0, pieces, step, 0)

    return serve, finish, close, local.wait


def link_semaphores(pieces):
    dma = pltpu.SemaphoreType.DMA
    return [dma, dma((pieces, 8)), dma((pieces, 8)), dma((pieces, 8)), dma((pieces, 8)),
            dma((pieces, 3)), dma((pieces, 2, 4)), dma((pieces, 8)), dma((pieces, 8)), dma((pieces, 8))]


def gelu_norm(values, gain, width):
    square = jnp.sum(values * values, axis=1, keepdims=True) * (1.0 / width)
    v = values * lax.rsqrt(square + 1e-06) * gain
    u = v * (0.7978845608028654 + (0.7978845608028654 * 0.044715) * (v * v))
    h = 0.5 * v
    return h + h * jnp.tanh(u)


def unet_kernel(dims, pieces, g_ref, hot_ref, sw_ref, mask_ref, gain0_ref, gain1_ref, gain2_ref, head_ref,
                out_ref, logit_ref, gv, sems, wide, pf, pb1, pb2, skip0, skip1, skip2, mix, *links):
    rows, c0, c1, c2, offs = dims
    ext = rows + 2 * HALO
    w0, w1 = c0 // 8, c1 // 8
    cuts = list(zip(offs[:-1], offs[1:]))

    if pieces:
        serve, finish, close, wait_local = link_steps(pieces, g_ref, gv, links)
    else:
        def serve(m):
            return None

        def load(n):
            lo, hi = cuts[n]
            return pltpu.make_async_copy(
                g_ref.at[:, pl.ds(lo, hi - lo), :], gv.at[:, pl.ds(lo, hi - lo), :], sems.at[n])

        for n in range(5):
            load(n).start()

    served = [0, 0]

    def need(n):
        if not pieces:
            load(n).wait()
            return
        if served[1] == 0:
            wait_local()
        last = min(-(-cuts[n][1] // PIECE), pieces)
        if last > served[1]:
            until = (last + 6) * 6

            def step(m, carry):
                serve(m)
                return carry

            if until > served[0]:
                lax.fori_loop(served[0], until, step, 0)
                served[0] = until
            finish(served[1], last)
            served[1] = last

    def chunks(count, body, at=None):
        def step(i, carry):
            body(pl.multiple_of(i * CHUNK, CHUNK))
            if at is not None:
                at(i)
            return carry
        lax.fori_loop(0, count // CHUNK, step, 0)

    def shifted(k, start, shift, width):
        if shift == 0:
            return pf[k, pl.ds(start, CHUNK), 0:width].astype(BF16)
        if shift < 0:
            return pf[k, pl.ds(start - 8, CHUNK + 8), 0:width][7:7 + CHUNK].astype(BF16)
        return pf[k, pl.ds(start, CHUNK + 8), 0:width][1:1 + CHUNK].astype(BF16)

    zeros = jnp.zeros((8, pf.shape[2]), F32)
    for k in range(4):
        pf[k, 0:8, :] = zeros
        pf[k, 8 + ext:16 + ext, :] = zeros

    def stem(j, carry):
        for e in range(2):
            wide[e, :, 0:c0] = jnp.dot(hot_ref[...], sw_ref[2 * j + e], preferred_element_type=F32)

        def body(r):
            a0 = gelu_norm(wide[0, pl.ds(r, CHUNK), 0:c0], gain0_ref[...], c0)
            a1 = gelu_norm(wide[1, pl.ds(r, CHUNK), 0:c0], gain0_ref[...], c0)
            skip0[2 * j, pl.ds(r, CHUNK), :] = a0.astype(BF16)
            skip0[2 * j + 1, pl.ds(r, CHUNK), :] = a1.astype(BF16)
            pf[j, pl.ds(r + 8, CHUNK), 0:c0] = 0.5 * (a0 + a1) * mask_ref[pl.ds(r, CHUNK), 0:1]

        chunks(ext, body, lambda i: serve(j * (ext // CHUNK) + i))
        return carry

    lax.fori_loop(0, 4, stem, 0)
    served[0] = 4 * (ext // CHUNK)

    where1 = {(k, 0): k for k in range(4)} | {(2, -1): 4, (3, -1): 5, (0, 1): 6, (1, 1): 7}
    for (k, shift), at in where1.items():
        def body(r, k=k, shift=shift, at=at):
            pb1[at, pl.ds(r, CHUNK), :] = shifted(k, r + 8, shift, c0)
        chunks(ext, body)

    need(0)
    for j in range(2):
        for e in range(2):
            k = 2 * j + e

            def column(p, carry, k=k, e=e, m=served[0]):
                serve(m + p)
                acc = None
                for t in range(TAPS):
                    shift, cls = divmod(k + t - 2, 4)
                    term = jnp.dot(pb1[where1[(cls, shift)]], gv[p, offs[0] + t * c0:offs[0] + (t + 1) * c0, :],
                                   preferred_element_type=F32)
                    acc = term if acc is None else acc + term
                wide[e, :, pl.ds(pl.multiple_of(p * 256, 256), 256)] = acc
                return carry

            lax.fori_loop(0, 4, column, 0)
            served[0] += 4

        def body(r, j=j):
            both = []
            for e in range(2):
                row = wide[e, pl.ds(r, CHUNK), :]
                row = jnp.concatenate([row[:, s * LANES:s * LANES + w1] for s in range(8)], axis=1)
                a = gelu_norm(row, gain1_ref[...], c1)
                skip1[2 * j + e, pl.ds(r, CHUNK), :] = a.astype(BF16)
                both.append(a)
            pf[j, pl.ds(r + 8, CHUNK), 0:c1] = 0.5 * (both[0] + both[1]) * mask_ref[pl.ds(r, CHUNK), 0:1]

        first = served[0]
        chunks(ext, body, lambda i: pl.when(i % 2 == 0)(lambda: serve(first + i // 2)))
        served[0] += (ext // CHUNK + 1) // 2

    where2 = {}
    for k in range(2):
        for shift in (-1, 0, 1):
            at = len(where2)
            where2[(k, shift)] = at

            def body(r, k=k, shift=shift, at=at):
                pb2[at, pl.ds(r, CHUNK), :] = shifted(k, r + 8 + HALO, shift, c1)

            chunks(rows, body)

    need(1)
    for e in range(2):
        def column(p, carry, e=e):
            acc = None
            for t in range(TAPS):
                shift, cls = divmod(e + t - 2, 2)
                term = jnp.dot(pb2[where2[(cls, shift)]], gv[p, offs[1] + t * c1:offs[1] + (t + 1) * c1, :],
                               preferred_element_type=F32)
                acc = term if acc is None else acc + term
            wide[e, 0:rows, pl.ds(pl.multiple_of(p * 256, 256), 256)] = acc
            return carry

        lax.fori_loop(0, 4, column, 0)

    def body(r):
        a0 = gelu_norm(wide[0, pl.ds(r, CHUNK), :], gain2_ref[...], c2)
        a1 = gelu_norm(wide[1, pl.ds(r, CHUNK), :], gain2_ref[...], c2)
        skip2[0, pl.ds(r, CHUNK), :] = a0.astype(BF16)
        skip2[1, pl.ds(r, CHUNK), :] = a1.astype(BF16)
        skip2[2, pl.ds(r, CHUNK), :] = (0.5 * (a0 + a1)).astype(BF16)

    first = served[0]
    chunks(rows, body, lambda i: serve(first + i))
    served[0] += rows // CHUNK

    def lift(slot, lhs, n, depth):
        def column(p, carry):
            wide[slot, 0:rows, pl.ds(pl.multiple_of(p * 256, 256), 256)] = jnp.dot(
                lhs(), gv[p, offs[n]:offs[n] + depth, :], preferred_element_type=F32)
            return carry
        lax.fori_loop(0, 4, column, 0)

    need(2)
    lift(0, lambda: skip2[2], 2, c2)

    def body(r):
        up = wide[0, pl.ds(r, CHUNK), :]
        for e in range(2):
            skip2[e, pl.ds(r, CHUNK), :] = (skip2[e, pl.ds(r, CHUNK), :].astype(F32) + up).astype(BF16)

    chunks(rows, body)

    need(3)

    def middle(j, carry):
        lift(0, lambda: skip2[j], 3, c2)

        def body(r):
            row = wide[0, pl.ds(r, CHUNK), :]
            up = jnp.concatenate([row[:, s * LANES:s * LANES + w1] for s in range(8)], axis=1)
            for e in range(2):
                at = pl.ds(r + HALO, CHUNK)
                skip1[2 * j + e, at, :] = (skip1[2 * j + e, at, :].astype(F32) + up).astype(BF16)

        chunks(rows, body)
        return carry

    lax.fori_loop(0, 2, middle, 0)

    need(4)

    def top(j, carry):
        lift(0, lambda: skip1[j, HALO:HALO + rows, :], 4, c1)

        def body(r):
            row = wide[0, pl.ds(r, CHUNK), :]
            up = jnp.concatenate([row[:, s * LANES:s * LANES + w0] for s in range(8)], axis=1)
            pf[j, pl.ds(r, CHUNK), 0:c0] = up

        chunks(rows, body)
        return carry

    lax.fori_loop(0, 4, top, 0)

    def final(i, carry):
        r = pl.multiple_of(i * 16, 16)
        for j in range(4):
            up = pf[j, pl.ds(r, 16), 0:c0]
            for e in range(2):
                k = 2 * j + e
                f = skip0[k, pl.ds(r + HALO, 16), :].astype(F32) + up
                for lane in range(0, c0, LANES):
                    mix[lane // LANES, pl.ds(k, 16, stride=8), :] = f[:, lane:lane + LANES]
        o = pl.multiple_of(i * 128, 128)
        for lane in range(0, c0, LANES):
            out_ref[pl.ds(o, 128), lane:lane + LANES] = mix[lane // LANES].astype(BF16)
        logits = lax.dot_general(head_ref[...], out_ref[pl.ds(o, 128), :], (((1,), (1,)), ((), ())),
                                 preferred_element_type=F32)
        logit_ref[:, pl.ds(o, 128)] = logits[0:logit_ref.shape[0]]
        return carry

    lax.fori_loop(0, rows // 16, final, 0)
    if pieces:
        close()


def unet(g, pieces, hot, sw, mask, gain0, gain1, gain2, head, dims, classes):
    rows, c0, c1, c2, offs = dims
    ext = rows + 2 * HALO
    vmem = pl.BlockSpec(memory_space=pltpu.VMEM)
    head = jnp.pad(head.T, ((0, 16 - classes), (0, 0)))
    return pl.pallas_call(
        functools.partial(unet_kernel, dims, pieces),
        out_shape=(jax.ShapeDtypeStruct((rows * 8, c0), BF16), jax.ShapeDtypeStruct((classes, rows * 8), F32)),
        in_specs=[pl.BlockSpec(memory_space=pl.ANY)] + [vmem] * 7,
        out_specs=(vmem, vmem),
        scratch_shapes=[
            pltpu.VMEM((4, offs[-1], 2 * LANES), BF16),
            pltpu.SemaphoreType.DMA((5,)),
            pltpu.VMEM((2, ext, 1024), F32),
            pltpu.VMEM((4, ext + 16, c1), F32),
            pltpu.VMEM((8, ext, c0), BF16),
            pltpu.VMEM((6, rows, c1), BF16),
            pltpu.VMEM((8, ext, c0), BF16),
            pltpu.VMEM((4, ext, c1), BF16),
            pltpu.VMEM((3, rows, c2), BF16),
            pltpu.VMEM((c0 // LANES, 128, LANES), F32),
        ] + (link_semaphores(pieces) if pieces else []),
        compiler_params=pltpu.CompilerParams(
            **(dict(collective_id=0, has_side_effects=True) if pieces else {}),
            vmem_limit_bytes=64 * 1024 * 1024 - 512 * 1024),
        name="unet",
    )(g, hot, sw, mask, gain0[None], gain1[None], gain2[None], head)


def flat(weight):
    weight = weight.reshape(-1, weight.shape[-1])
    return jnp.pad(weight, ((0, 0), (0, LANES - weight.shape[-1])))


def solution(mesh):
    chips = mesh.shape["seq"] == 8 and mesh.shape["dp"] == 4

    def on_device(bases, stem_weight, stem_gain, first_weight, first_gain, second_weight, second_gain,
                  bottom_project, middle_project, top_project, head_weight):
        weights = (first_weight, second_weight, bottom_project, middle_project, top_project)
        depths = [w.size // w.shape[-1] for w in weights]
        offs = [0]
        for d in depths:
            offs.append(offs[-1] + d)
        if chips and offs[-1] % PIECE == 0:
            pieces = offs[-1] // PIECE
            g = jnp.concatenate([flat(w) for w in weights], axis=0)
        else:
            pieces = 0
            parts = []
            for w in weights:
                whole = lax.all_gather(w.reshape(-1, w.shape[-1]), "seq", axis=1, tiled=True)
                whole = whole.reshape(whole.shape[0], 8, -1)
                whole = jnp.pad(whole, ((0, 0), (0, 0), (0, LANES - whole.shape[2])))
                parts.append(whole.reshape(-1, 4, 2 * LANES).transpose(1, 0, 2))
            g = jnp.concatenate(parts, axis=1)

        count = lax.axis_size("seq")
        me = lax.axis_index("seq")
        length = bases.shape[0]
        rows = length // CLASSES
        ext = rows + 2 * HALO
        forward = [(i, i + 1) for i in range(count - 1)]
        low = lax.ppermute(bases[-16:] + 1, "seq", forward) - 1
        high = lax.ppermute(bases[:16] + 1, "seq", [(b, a) for a, b in forward]) - 1
        blank = jnp.full((8 * (HALO + 1) - 16,), -1, jnp.int32)
        line = jnp.concatenate([blank, low, bases, high, blank]).reshape(ext + 2, 8)
        window = jnp.concatenate([line[:-2, 6:], line[1:-1], line[2:, :2]], axis=1)
        lane = jnp.arange(48, dtype=jnp.int32)
        hot = (jnp.repeat(window, 4, axis=1) == (lane % 4)[None]).astype(BF16)
        at = jnp.arange(8 * 48, dtype=jnp.int32)[:, None]
        pick = (at % 48 - 4 * (at // 48) == jnp.arange(20, dtype=jnp.int32)[None]).astype(BF16)
        sw = jnp.dot(pick, stem_weight, preferred_element_type=F32).astype(BF16).reshape(8, 48, -1)
        q = jnp.arange(ext)[:, None]
        outside = ((me == 0) & (q < HALO)) | ((me == count - 1) & (q >= HALO + rows))
        mask = jnp.broadcast_to(jnp.where(outside, 0.0, 1.0).astype(F32), (ext, LANES))
        dims = (rows, stem_weight.shape[1], first_gain.shape[0], second_gain.shape[0], tuple(offs))
        return unet(g, pieces, hot, sw, mask, stem_gain, first_gain, second_gain, head_weight, dims, head_weight.shape[1])

    placed = (
        P(("dp", "seq")),
        P(),
        P(),
        P(None, None, "seq"),
        P(),
        P(None, None, "seq"),
        P(),
        P(None, "seq"),
        P(None, "seq"),
        P(None, "seq"),
        P(),
    )
    return jax.shard_map(
        on_device,
        mesh=mesh,
        in_specs=placed,
        out_specs=(P(("dp", "seq"), None), P(None, ("dp", "seq"))),
        check_vma=False,
    )
```

```python
import functools

import jax
import jax.numpy as jnp
from jax import lax
from jax.experimental import pallas as pl
from jax.experimental.pallas import tpu as pltpu
from jax.sharding import PartitionSpec as P

TAPS = 5
CLASSES = 8
HALO = 16
CHUNK = 32
LANES = 128
PIECE = 1024
AHEAD = 1
SPLIT = 1
BF16 = jnp.bfloat16
F32 = jnp.float32


def link_steps(pieces, x_ref, g_ref, sems):
    (local_sem, nat_recv, x_recv, ca_recv, cb_recv, own_send, nat_send, x_send, ca_send, cb_send) = sems
    seq = lax.axis_index("seq")
    dp = lax.axis_index("dp")
    z, y = seq // 2, seq % 2
    x, c = dp // 2, dp % 2
    half = PIECE // 2
    edge = half * 3 // 8 // 16 * 16
    native = half - edge

    def there(zz, yy, xx, cc):
        return {"seq": zz * 2 + yy, "dp": xx * 2 + cc}

    y_dev = there(z, 1 - y, x, c)
    x_dev = there(z, y, 1 - x, c)
    c_dev = there(z, y, x, 1 - c)
    up_dev = there(jnp.minimum(z + 1, 3), y, x, c)
    down_dev = there(jnp.maximum(z - 1, 0), y, x, c)

    barrier = pltpu.get_barrier_semaphore()
    for dev in (y_dev, x_dev, c_dev):
        pl.semaphore_signal(barrier, inc=1, device_id=dev, device_id_type=pl.DeviceIdType.MESH)

    @pl.when(z < 3)
    def _():
        pl.semaphore_signal(barrier, inc=1, device_id=up_dev, device_id_type=pl.DeviceIdType.MESH)

    @pl.when(z > 0)
    def _():
        pl.semaphore_signal(barrier, inc=1, device_id=down_dev, device_id_type=pl.DeviceIdType.MESH)

    inner = jnp.logical_and(z > 0, z < 3)

    @pl.when(inner)
    def _():
        pl.semaphore_wait(barrier, 5)

    @pl.when(jnp.logical_not(inner))
    def _():
        pl.semaphore_wait(barrier, 4)

    def slot(zz, yy, start, count):
        return g_ref.at[zz, pl.ds(pl.multiple_of(start, 16), count),
                        pl.ds(pl.multiple_of(yy * LANES, LANES), LANES)]

    def base(k):
        return k * PIECE + c * half

    def copy(src, dst, send, recv, dev):
        return pltpu.make_async_remote_copy(src_ref=src, dst_ref=dst, send_sem=send, recv_sem=recv,
                                            device_id=dev, device_id_type=pl.DeviceIdType.MESH)

    def nat(k, zz, yy):
        return slot(zz, yy, base(k) + x * edge, native)

    def part(k, zz, yy, xx):
        return slot(zz, yy, base(k) + xx * native, edge)

    def own_copy(k, dev, which):
        src = x_ref.at[pl.ds(pl.multiple_of(base(k) + x * edge, 16), native), :]
        return copy(src, nat(k, z, y), own_send.at[k, which], nat_recv.at[k, seq], dev)

    def z_copy(k, zz, dev):
        s = zz * 2 + y
        return copy(nat(k, zz, y), nat(k, zz, y), nat_send.at[k, 0, zz], nat_recv.at[k, s], dev)

    def y_copy(k, zz):
        s = zz * 2 + y
        return copy(nat(k, zz, y), nat(k, zz, y), nat_send.at[k, 1, zz], nat_recv.at[k, s], y_dev)

    def x_copy(k, zz, yy):
        s = zz * 2 + yy
        return copy(part(k, zz, yy, x), part(k, zz, yy, x), x_send.at[k, s], x_recv.at[k, s], x_dev)

    def ca_copy(k, zz, yy):
        s = zz * 2 + yy
        return copy(nat(k, zz, yy), nat(k, zz, yy), ca_send.at[k, s], ca_recv.at[k, s], c_dev)

    def cb_copy(k, zz, yy):
        s = zz * 2 + yy
        return copy(part(k, zz, yy, 1 - x), part(k, zz, yy, 1 - x), cb_send.at[k, s], cb_recv.at[k, s], c_dev)

    local = pltpu.make_async_copy(
        x_ref, g_ref.at[z, :, pl.ds(pl.multiple_of(y * LANES, LANES), LANES)], local_sem)
    local.start()

    def wait_nat(k, zz, yy):
        pltpu.make_async_copy(nat(k, zz, yy), nat(k, zz, yy), nat_recv.at[k, zz * 2 + yy]).wait()

    def wait_part(k, zz, yy, sem):
        ref = part(k, zz, yy, 1 - x)
        pltpu.make_async_copy(ref, ref, sem.at[k, zz * 2 + yy]).wait()

    def start_own(k):
        pl.when(z < 3)(lambda: own_copy(k, up_dev, 0).start())
        pl.when(z > 0)(lambda: own_copy(k, down_dev, 1).start())
        own_copy(k, y_dev, 2).start()

    def serve(m):
        n, i = m // 6, m % 6
        phase = (6 - i) % 6
        k = n - phase - AHEAD * jnp.minimum(phase, 1)

        def inside(zz):
            return jnp.logical_and(zz >= 0, zz < 4)

        @pl.when(jnp.logical_and(k >= 0, k < pieces))
        def _():
            @pl.when(phase == 0)
            def _():
                start_own(k)

            @pl.when(phase > 0)
            def _():
                for sign in (-1, 1):
                    zz = z + sign * phase

                    @pl.when(inside(zz))
                    def _(zz=zz, sign=sign):
                        wait_nat(k, zz, y)
                        if sign < 0:
                            pl.when(z < 3)(lambda: z_copy(k, zz, up_dev).start())
                        else:
                            pl.when(z > 0)(lambda: z_copy(k, zz, down_dev).start())
                        y_copy(k, zz).start()
                        x_copy(k, zz, y).start()
                        ca_copy(k, zz, y).start()
                for sign in (-1, 1):
                    zz = z + sign * (phase - 1)

                    @pl.when(jnp.logical_and(inside(zz), phase > (1 if sign < 0 else 0)))
                    def _(zz=zz):
                        wait_nat(k, zz, 1 - y)
                        x_copy(k, zz, 1 - y).start()
                        ca_copy(k, zz, 1 - y).start()
                for sign in (-1, 1):
                    zz = z + sign * (phase - 1)

                    @pl.when(jnp.logical_and(inside(zz), phase > 1))
                    def _(zz=zz):
                        wait_part(k, zz, y, x_recv)
                        cb_copy(k, zz, y).start()
                for sign in (-1, 1):
                    zz = z + sign * (phase - 2)

                    @pl.when(jnp.logical_and(inside(zz), phase > (2 if sign < 0 else 1)))
                    def _(zz=zz):
                        wait_part(k, zz, 1 - y, x_recv)
                        cb_copy(k, zz, 1 - y).start()

    def finish(lo, hi):
        def step(k, carry):
            def shard(s, carry):
                @pl.when(s != seq)
                def _():
                    zz, yy = s // 2, s % 2
                    start = k * PIECE + (1 - c) * half
                    got = slot(zz, yy, start + x * edge, native)
                    pltpu.make_async_copy(got, got, ca_recv.at[k, s]).wait()
                    got = slot(zz, yy, start + (1 - x) * native, edge)
                    pltpu.make_async_copy(got, got, cb_recv.at[k, s]).wait()
                return carry
            return lax.fori_loop(0, 8, shard, carry)
        lax.fori_loop(lo, hi, step, 0)

    def close(lo, hi):
        def step(k, carry):
            pl.when(z < 3)(lambda: own_copy(k, up_dev, 0).wait_send())
            pl.when(z > 0)(lambda: own_copy(k, down_dev, 1).wait_send())
            own_copy(k, y_dev, 2).wait_send()

            def shard(s, carry):
                zz, yy = s // 2, s % 2

                @pl.when(s != seq)
                def _():
                    x_copy(k, zz, yy).wait_send()
                    ca_copy(k, zz, yy).wait_send()
                    cb_copy(k, zz, yy).wait_send()

                @pl.when(jnp.logical_and(zz != z, yy == 0))
                def _():
                    pl.when(jnp.logical_and(zz < z, z < 3))(lambda: z_copy(k, zz, up_dev).wait_send())
                    pl.when(jnp.logical_and(zz > z, z > 0))(lambda: z_copy(k, zz, down_dev).wait_send())
                    y_copy(k, zz).wait_send()
                return carry
            return lax.fori_loop(0, 8, shard, carry)
        lax.fori_loop(lo, hi, step, 0)

    return serve, finish, close, local.wait


def link_semaphores(pieces):
    dma = pltpu.SemaphoreType.DMA
    return [dma, dma((pieces, 8)), dma((pieces, 8)), dma((pieces, 8)), dma((pieces, 8)),
            dma((pieces, 3)), dma((pieces, 2, 4)), dma((pieces, 8)), dma((pieces, 8)), dma((pieces, 8))]


def gelu_norm(values, gain, width):
    square = jnp.sum(values * values, axis=1, keepdims=True) * (1.0 / width)
    v = values * lax.rsqrt(square + 1e-06) * gain
    u = v * (0.7978845608028654 + (0.7978845608028654 * 0.044715) * (v * v))
    h = 0.5 * v
    return h + h * jnp.tanh(u)


def unet_kernel(dims, pieces, g_ref, hot_ref, sw_ref, gain_ref, head_ref,
                out_ref, logit_ref, gv, sems, wide, pf, pb1, pb2, skip0, skip1, skip2, mix, *links):
    rows, c0, c1, c2, offs = dims
    ext = rows + 2 * HALO
    w0, w1 = c0 // 8, c1 // 8
    cuts = list(zip(offs[:-1], offs[1:]))

    if pieces:
        serve_one, finish, close, wait_local = link_steps(pieces, g_ref, gv, links)

        def serve(m):
            if SPLIT == 1:
                serve_one(m)
                return

            def one(i, carry):
                serve_one(m * SPLIT + i)
                return carry

            lax.fori_loop(0, SPLIT, one, 0)
    else:
        def serve(m):
            return None

        def load(n):
            lo, hi = cuts[n]
            return pltpu.make_async_copy(
                g_ref.at[:, pl.ds(lo, hi - lo), :], gv.at[:, pl.ds(lo, hi - lo), :], sems.at[n])

        for n in range(5):
            load(n).start()

    served = [0, 0, 0]

    def need(n):
        if not pieces:
            load(n).wait()
            return
        if served[1] == 0:
            wait_local()
        elif n <= 2:
            close(served[2], served[1])
            served[2] = served[1]
        last = min(-(-cuts[n][1] // PIECE), pieces)
        if last > served[1]:
            until = -(-(last + 5 + AHEAD) * 6 // SPLIT)

            def step(m, carry):
                serve(m)
                return carry

            if until > served[0]:
                lax.fori_loop(served[0], until, step, 0)
                served[0] = until
            finish(served[1], last)
            served[1] = last

    def chunks(count, body, at=None):
        def step(i, carry):
            body(pl.multiple_of(i * CHUNK, CHUNK))
            if at is not None:
                at(i)
            return carry
        lax.fori_loop(0, count // CHUNK, step, 0)

    me = lax.axis_index("seq")
    low = jnp.where(me == 0, HALO, 0)
    high = jnp.where(me == lax.axis_size("seq") - 1, HALO + rows, ext)

    def inside(r):
        at = r + lax.broadcasted_iota(jnp.int32, (CHUNK, 1), 0)
        return jnp.where(jnp.logical_and(at >= low, at < high), 1.0, 0.0)

    def shifted(k, start, shift, width):
        if shift == 0:
            return pf[k, pl.ds(start, CHUNK), 0:width].astype(BF16)
        if shift < 0:
            return pf[k, pl.ds(start - 8, CHUNK + 8), 0:width][7:7 + CHUNK].astype(BF16)
        return pf[k, pl.ds(start, CHUNK + 8), 0:width][1:1 + CHUNK].astype(BF16)

    zeros = jnp.zeros((8, pf.shape[2]), F32)
    for k in range(4):
        pf[k, 0:8, :] = zeros
        pf[k, 8 + ext:16 + ext, :] = zeros

    def stem(j, carry):
        for e in range(2):
            wide[e, :, 0:c0] = jnp.dot(hot_ref[...], sw_ref[2 * j + e], preferred_element_type=F32)

        def body(r):
            a0 = gelu_norm(wide[0, pl.ds(r, CHUNK), 0:c0], gain_ref[:, 0:c0], c0)
            a1 = gelu_norm(wide[1, pl.ds(r, CHUNK), 0:c0], gain_ref[:, 0:c0], c0)
            skip0[2 * j, pl.ds(r, CHUNK), :] = a0.astype(BF16)
            skip0[2 * j + 1, pl.ds(r, CHUNK), :] = a1.astype(BF16)
            pf[j, pl.ds(r + 8, CHUNK), 0:c0] = 0.5 * (a0 + a1) * inside(r)

        chunks(ext, body, lambda i: serve(j * (ext // CHUNK) + i))
        return carry

    lax.fori_loop(0, 4, stem, 0)
    served[0] = 4 * (ext // CHUNK)

    where1 = {(k, 0): k for k in range(4)} | {(2, -1): 4, (3, -1): 5, (0, 1): 6, (1, 1): 7}
    for (k, shift), at in where1.items():
        def body(r, k=k, shift=shift, at=at):
            pb1[at, pl.ds(r, CHUNK), :] = shifted(k, r + 8, shift, c0)
        chunks(ext, body)

    need(0)
    for j in range(2):
        for e in range(2):
            k = 2 * j + e

            def column(p, carry, k=k, e=e, m=served[0]):
                serve(m + p)
                acc = None
                for t in range(TAPS):
                    shift, cls = divmod(k + t - 2, 4)
                    term = jnp.dot(pb1[where1[(cls, shift)]], gv[p, offs[0] + t * c0:offs[0] + (t + 1) * c0, :],
                                   preferred_element_type=F32)
                    acc = term if acc is None else acc + term
                wide[e, :, pl.ds(pl.multiple_of(p * 256, 256), 256)] = acc
                return carry

            lax.fori_loop(0, 4, column, 0)
            served[0] += 4

        def body(r, j=j):
            both = []
            for e in range(2):
                row = wide[e, pl.ds(r, CHUNK), :]
                row = jnp.concatenate([row[:, s * LANES:s * LANES + w1] for s in range(8)], axis=1)
                a = gelu_norm(row, gain_ref[:, c0:c0 + c1], c1)
                skip1[2 * j + e, pl.ds(r, CHUNK), :] = a.astype(BF16)
                both.append(a)
            pf[j, pl.ds(r + 8, CHUNK), 0:c1] = 0.5 * (both[0] + both[1]) * inside(r)

        first = served[0]
        chunks(ext, body, lambda i: pl.when(i % 2 == 0)(lambda: serve(first + i // 2)))
        served[0] += (ext // CHUNK + 1) // 2

    where2 = {}
    for k in range(2):
        for shift in (-1, 0, 1):
            at = len(where2)
            where2[(k, shift)] = at

            def body(r, k=k, shift=shift, at=at):
                pb2[at, pl.ds(r, CHUNK), :] = shifted(k, r + 8 + HALO, shift, c1)

            chunks(rows, body)

    need(1)
    for e in range(2):
        def column(p, carry, e=e):
            acc = None
            for t in range(TAPS):
                shift, cls = divmod(e + t - 2, 2)
                term = jnp.dot(pb2[where2[(cls, shift)]], gv[p, offs[1] + t * c1:offs[1] + (t + 1) * c1, :],
                               preferred_element_type=F32)
                acc = term if acc is None else acc + term
            wide[e, 0:rows, pl.ds(pl.multiple_of(p * 256, 256), 256)] = acc
            return carry

        lax.fori_loop(0, 4, column, 0)

    def body(r):
        a0 = gelu_norm(wide[0, pl.ds(r, CHUNK), :], gain_ref[:, c0 + c1:c0 + c1 + c2], c2)
        a1 = gelu_norm(wide[1, pl.ds(r, CHUNK), :], gain_ref[:, c0 + c1:c0 + c1 + c2], c2)
        skip2[0, pl.ds(r, CHUNK), :] = a0.astype(BF16)
        skip2[1, pl.ds(r, CHUNK), :] = a1.astype(BF16)
        skip2[2, pl.ds(r, CHUNK), :] = (0.5 * (a0 + a1)).astype(BF16)

    first = served[0]
    chunks(rows, body, lambda i: serve(first + i))
    served[0] += rows // CHUNK

    def lift(slot, lhs, n, depth):
        def column(p, carry):
            wide[slot, 0:rows, pl.ds(pl.multiple_of(p * 256, 256), 256)] = jnp.dot(
                lhs(), gv[p, offs[n]:offs[n] + depth, :], preferred_element_type=F32)
            return carry
        lax.fori_loop(0, 4, column, 0)

    need(2)
    lift(0, lambda: skip2[2], 2, c2)

    def body(r):
        up = wide[0, pl.ds(r, CHUNK), :]
        for e in range(2):
            skip2[e, pl.ds(r, CHUNK), :] = (skip2[e, pl.ds(r, CHUNK), :].astype(F32) + up).astype(BF16)

    chunks(rows, body)

    need(3)

    def middle(j, carry):
        lift(0, lambda: skip2[j], 3, c2)

        def body(r):
            row = wide[0, pl.ds(r, CHUNK), :]
            up = jnp.concatenate([row[:, s * LANES:s * LANES + w1] for s in range(8)], axis=1)
            for e in range(2):
                at = pl.ds(r + HALO, CHUNK)
                skip1[2 * j + e, at, :] = (skip1[2 * j + e, at, :].astype(F32) + up).astype(BF16)

        chunks(rows, body)
        return carry

    lax.fori_loop(0, 2, middle, 0)

    need(4)

    def top(j, carry):
        lift(0, lambda: skip1[j, HALO:HALO + rows, :], 4, c1)

        def body(r):
            row = wide[0, pl.ds(r, CHUNK), :]
            up = jnp.concatenate([row[:, s * LANES:s * LANES + w0] for s in range(8)], axis=1)
            pf[j, pl.ds(r, CHUNK), 0:c0] = up

        chunks(rows, body)
        return carry

    lax.fori_loop(0, 4, top, 0)

    def final(i, carry):
        r = pl.multiple_of(i * 16, 16)
        for j in range(4):
            up = pf[j, pl.ds(r, 16), 0:c0]
            for e in range(2):
                k = 2 * j + e
                f = skip0[k, pl.ds(r + HALO, 16), :].astype(F32) + up
                for lane in range(0, c0, LANES):
                    mix[lane // LANES, pl.ds(k, 16, stride=8), :] = f[:, lane:lane + LANES]
        o = pl.multiple_of(i * 128, 128)
        for lane in range(0, c0, LANES):
            out_ref[pl.ds(o, 128), lane:lane + LANES] = mix[lane // LANES].astype(BF16)
        logits = lax.dot_general(head_ref[...], out_ref[pl.ds(o, 128), :], (((1,), (1,)), ((), ())),
                                 preferred_element_type=F32)
        logit_ref[:, pl.ds(o, 128)] = logits[0:logit_ref.shape[0]]
        return carry

    lax.fori_loop(0, rows // 16, final, 0)
    if pieces:
        close(served[2], pieces)


def unet(g, pieces, hot, sw, gains, head, dims, classes):
    rows, c0, c1, c2, offs = dims
    ext = rows + 2 * HALO
    vmem = pl.BlockSpec(memory_space=pltpu.VMEM)
    head = jnp.pad(head.T, ((0, 16 - classes), (0, 0)))
    return pl.pallas_call(
        functools.partial(unet_kernel, dims, pieces),
        out_shape=(jax.ShapeDtypeStruct((rows * 8, c0), BF16), jax.ShapeDtypeStruct((classes, rows * 8), F32)),
        in_specs=[pl.BlockSpec(memory_space=pl.ANY)] + [vmem] * 4,
        out_specs=(vmem, vmem),
        scratch_shapes=[
            pltpu.VMEM((4, offs[-1], 2 * LANES), BF16),
            pltpu.SemaphoreType.DMA((5,)),
            pltpu.VMEM((2, ext, 1024), F32),
            pltpu.VMEM((4, ext + 16, c1), F32),
            pltpu.VMEM((8, ext, c0), BF16),
            pltpu.VMEM((6, rows, c1), BF16),
            pltpu.VMEM((8, ext, c0), BF16),
            pltpu.VMEM((4, ext, c1), BF16),
            pltpu.VMEM((3, rows, c2), BF16),
            pltpu.VMEM((c0 // LANES, 128, LANES), F32),
        ] + (link_semaphores(pieces) if pieces else []),
        compiler_params=pltpu.CompilerParams(
            **(dict(collective_id=0, has_side_effects=True) if pieces else {}),
            vmem_limit_bytes=64 * 1024 * 1024 - 512 * 1024),
        name="unet",
    )(g, hot, sw, gains[None], head)


def flat(weight):
    weight = weight.reshape(-1, weight.shape[-1])
    return jnp.pad(weight, ((0, 0), (0, LANES - weight.shape[-1])))


def solution(mesh):
    chips = mesh.shape["seq"] == 8 and mesh.shape["dp"] == 4

    def on_device(bases, stem_weight, stem_gain, first_weight, first_gain, second_weight, second_gain,
                  bottom_project, middle_project, top_project, head_weight):
        weights = (first_weight, second_weight, bottom_project, middle_project, top_project)
        depths = [w.size // w.shape[-1] for w in weights]
        offs = [0]
        for d in depths:
            offs.append(offs[-1] + d)
        if chips and offs[-1] % PIECE == 0:
            pieces = offs[-1] // PIECE
            g = jnp.concatenate([flat(w) for w in weights], axis=0)
        else:
            pieces = 0
            parts = []
            for w in weights:
                whole = lax.all_gather(w.reshape(-1, w.shape[-1]), "seq", axis=1, tiled=True)
                whole = whole.reshape(whole.shape[0], 8, -1)
                whole = jnp.pad(whole, ((0, 0), (0, 0), (0, LANES - whole.shape[2])))
                parts.append(whole.reshape(-1, 4, 2 * LANES).transpose(1, 0, 2))
            g = jnp.concatenate(parts, axis=1)

        count = lax.axis_size("seq")
        length = bases.shape[0]
        rows = length // CLASSES
        ext = rows + 2 * HALO
        forward = [(i, i + 1) for i in range(count - 1)]
        low = lax.ppermute(bases[-16:] + 1, "seq", forward) - 1
        high = lax.ppermute(bases[:16] + 1, "seq", [(b, a) for a, b in forward]) - 1
        blank = jnp.full((8 * (HALO + 1) - 16,), -1, jnp.int32)
        line = jnp.concatenate([blank, low, bases, high, blank]).reshape(ext + 2, 8)
        window = jnp.concatenate([line[:-2, 6:], line[1:-1], line[2:, :2]], axis=1)
        lane = jnp.arange(48, dtype=jnp.int32)
        hot = (jnp.repeat(window, 4, axis=1) == (lane % 4)[None]).astype(BF16)
        at = jnp.arange(8 * 48, dtype=jnp.int32)[:, None]
        pick = (at % 48 - 4 * (at // 48) == jnp.arange(20, dtype=jnp.int32)[None]).astype(BF16)
        sw = jnp.dot(pick, stem_weight, preferred_element_type=F32).astype(BF16).reshape(8, 48, -1)
        dims = (rows, stem_weight.shape[1], first_gain.shape[0], second_gain.shape[0], tuple(offs))
        gains = jnp.concatenate([stem_gain, first_gain, second_gain])
        return unet(g, pieces, hot, sw, gains, head_weight, dims, head_weight.shape[1])

    placed = (
        P(("dp", "seq")),
        P(),
        P(),
        P(None, None, "seq"),
        P(),
        P(None, None, "seq"),
        P(),
        P(None, "seq"),
        P(None, "seq"),
        P(None, "seq"),
        P(),
    )
    return jax.shard_map(
        on_device,
        mesh=mesh,
        in_specs=placed,
        out_specs=(P(("dp", "seq"), None), P(None, ("dp", "seq"))),
        check_vma=False,
    )
```
